256 devices in a mesh: rows: 32 (over x, y, core), cls: 8 (over z).
Axes of the slice: x: 4, y: 4, z: 8, core: 2. Of those that a mesh axis runs over, the one named last changes fastest.
Arguments:
- features: float32 [8, 12288, 512], P('cls', 'rows'), may hold values from -6 to 6
- inverses: float32 [8, 512, 512], P('cls'), may hold values from -1 to 2
- weights: float32 [8, 512, 11264], P(None, 'rows', 'cls'), may hold values from -6 to 6
- residual: float32 [12288, 11264], P('rows', 'cls'), may hold values from -6 to 6
- order: int32 [3], replicated, may hold values from 0 to 7
- owner: int32 [8], replicated, may hold values from 0 to 7, each once
Outputs:
- weights_out: float32 [8, 512, 11264], P(None, 'rows', 'cls')
- residual_out: float32 [12288, 11264], P('rows', 'cls')
The draws below stay inside these ranges and needn't reach their ends.
Inputs may be any that keep to these rules, and one draw needn't show every extreme that they name: `owner`: each cls index stores exactly one block.
All inputs are finite; a program needn't handle non-finite values.
Results may differ from the reference program's by a relative error of at most 0.00013.
Values sent between devices are 32-bit elements; how exact they have to be, the bound alone decides.
A program may use at most 128 MiB of HBM per device.

```python
import jax
import jax.numpy as jnp
from jax import lax

BLOCK = 512
STEPS = 3
NBLK = 8
CLASSES = 11264
ROWS = 12288


def draw_inverses(key, part):
    first_key, second_key = jax.random.split(key)
    diagonal = jax.random.uniform(first_key, (NBLK, BLOCK), jnp.float32, 0.5, 1.5)
    jitter = jnp.clip(jax.random.normal(second_key, (NBLK, BLOCK, BLOCK), jnp.float32), -4.0, 4.0)
    jitter = jitter * (0.4 / BLOCK ** 0.5)
    symmetric = (jitter + jnp.swapaxes(jitter, 1, 2)) * 0.7071
    matrix = symmetric + jnp.eye(BLOCK, dtype=jnp.float32)[None, :, :] * diagonal[:, :, None]
    return matrix.astype(jnp.float32)


def spiked(array, key, source, target, parts, factor):
    owner, partner = [(jnp.arange(array.shape[axis_at]) // (array.shape[axis_at] // parts)).reshape([-1 if axis == axis_at else 1 for axis in range(array.ndim)]) for axis_at in (source, target)]
    chosen = jax.random.permutation(key, parts)[partner]
    strong = (owner == chosen) | (owner == (partner + parts // 2) % parts)
    return jnp.where(strong, factor * array, array)


def levels(own_key, extent, cuts, low, largest):
    factor_of, own = 1.0, jax.random.fold_in(own_key, 6)
    for position, parts in cuts:
        steps = jnp.exp(jax.random.uniform(jax.random.fold_in(own, position), (parts,), jnp.float32, low / len(cuts), largest / len(cuts)))
        factor_of = factor_of * jnp.repeat(steps, extent[position] // parts).reshape([-1 if axis == position else 1 for axis in range(len(extent))])
    return factor_of


def centred(key, extent, width, bound, shards=(), held_as=jnp.bfloat16):
    gain = levels(key, extent, shards, -0.22, 0.18) if shards else 1.0
    entries = jax.random.normal(key, extent, jnp.float32) * width * gain
    return jnp.minimum(jnp.maximum(entries, -bound), bound).astype(held_as)


def heavy_noise(rng, dims, width, most, cuts, heavy, held_as=jnp.bfloat16):
    result = width * jax.random.normal(rng, dims, jnp.float32)
    if cuts:
        result = result * levels(rng, dims, cuts, -0.22, 0.18)
    return jnp.clip(spiked(result, jax.random.fold_in(rng, 3), *heavy), -most, most).astype(held_as)


def setup_inputs(seed: int = 0) -> dict:
    key_of = jax.random.split(jax.random.key(seed), 7)
    features = heavy_noise(key_of[0], (NBLK, ROWS, BLOCK), 1.0, 6.0, ((0, 8), (1, 32)), (1, 2, 32, 2.75), jnp.float32)
    inverses = draw_inverses(jax.random.fold_in(key_of[6], 71), 0)
    weights = centred(key_of[2], (NBLK, BLOCK, CLASSES), 1.0, 6.0, ((1, 32), (2, 8)), jnp.float32)
    residual = centred(key_of[3], (ROWS, CLASSES), 1.0, 6.0, ((0, 32), (1, 8)), jnp.float32)
    order = jax.random.randint(key_of[4], (STEPS,), 0, NBLK).astype(jnp.int32)
    owner = jax.random.permutation(key_of[5], NBLK).astype(jnp.int32)
    return {"features": features, "inverses": inverses, "weights": weights, "residual": residual, "order": order, "owner": owner}


def reference(features, inverses, weights, residual, order, owner):
    penalty = ROWS / 64.0
    inv_rows = 1.0 / ROWS
    highest = lax.Precision.HIGHEST
    for iteration in range(STEPS):
        chosen = order[iteration].astype(jnp.int32)
        holder = owner[chosen].astype(jnp.int32)
        columns = lax.dynamic_index_in_dim(features, holder, 0, keepdims=False)
        inverse = lax.dynamic_index_in_dim(inverses, holder, 0, keepdims=False)
        current = lax.dynamic_index_in_dim(weights, chosen, 0, keepdims=False)
        correlation = lax.dot_general(columns, residual, (((0,), (0,)), ((), ())), precision=highest, preferred_element_type=jnp.float32)
        target = correlation - penalty * current
        change = jnp.dot(inverse, target, precision=highest, preferred_element_type=jnp.float32) * inv_rows
        weights = lax.dynamic_update_index_in_dim(weights, current + change, chosen, 0)
        residual = residual - jnp.dot(columns, change, precision=highest, preferred_element_type=jnp.float32)
    return weights, residual
```

```python
import functools

import jax
import jax.numpy as jnp
from jax import lax
from jax.experimental import pallas as pl
from jax.experimental.pallas import tpu as pltpu
from jax.sharding import PartitionSpec as P

STEPS = 3
MESH = pl.DeviceIdType.MESH
F32 = jnp.float32
BF16 = jnp.bfloat16


def split(value):
    high = value.astype(BF16)
    return high, (value - high.astype(F32)).astype(BF16)


def plan(chip_rows):
    eighths = chip_rows // 8
    first = (eighths + 1) // 2
    return (8 * first, 8 * (eighths - first))


def kernel(side, depth, parts, chosen_ref, holder_ref, x_ref, f_ref, i_ref, out_ref, *scratch):
    count = len(parts)
    (pz, stage, fbuf, iz, invf, wide, wide_low, wide_back, inv_high, inv_low) = scratch[:10]
    (z_send, z_recv, i_send, i_recv, c_send, c_recv, t_send, t_recv) = scratch[10:18]
    per_part = scratch[18:]
    cbuf, cother, rs1x, rs1y, t1x, t1y, rs2x, rs2y, tfull, dfull = (
        per_part[k * count : (k + 1) * count] for k in range(10)
    )
    rows = f_ref.shape[0]
    half = f_ref.shape[1] // 2
    quarter = half // 2
    total_rows = rows * side * side * 2
    penalty = total_rows / 64.0
    inv_rows = 1.0 / total_rows
    share = i_ref.shape[0]
    piece = rows // depth

    r = lax.axis_index("rows")
    mz = lax.axis_index("cls")
    core = lax.rem(r, 2)
    other = 1 - core
    my = lax.rem(lax.div(r, 2), side)
    mx = lax.div(r, 2 * side)

    def at_x(d):
        return ((lax.rem(mx + d, side) * side + my) * 2 + core, mz)

    def at_y(d):
        return ((mx * side + lax.rem(my + d, side)) * 2 + core, mz)

    def at_z(d):
        return (r, lax.rem(mz + d, depth))

    partner = ((mx * side + my) * 2 + other, mz)

    barrier = pltpu.get_barrier_semaphore()
    peers = (
        [at_x(d) for d in range(1, side)]
        + [at_y(d) for d in range(1, side)]
        + [at_z(d) for d in range(1, depth)]
        + [partner]
    )
    for peer in peers:
        pl.semaphore_signal(barrier, inc=1, device_id=peer, device_id_type=MESH)
    pl.semaphore_wait(barrier, len(peers))

    def remote(src, dst, send, recv, device):
        copy = pltpu.make_async_remote_copy(
            src_ref=src, dst_ref=dst, send_sem=send, recv_sem=recv, device_id=device, device_id_type=MESH
        )
        copy.start()
        return copy

    def finish(copies):
        for copy in copies:
            copy.wait()

    first_copies, inverse_copies = [], []
    for d in range(1, depth):
        to = lax.rem(mz + d, depth)
        first_copies.append(
            remote(f_ref.at[pl.ds(to * piece, piece)], pz.at[mz], z_send.at[0, d - 1], z_recv.at[0, d - 1], at_z(d))
        )
    for d in range(1, depth):
        inverse_copies.append(remote(i_ref, iz.at[mz], z_send.at[1, d - 1], z_recv.at[1, d - 1], at_z(d)))
    pz[mz] = f_ref[pl.ds(mz * piece, piece)]
    iz[mz] = i_ref[...]
    out_ref[...] = x_ref[...]
    finish(first_copies)

    def send_block(s):
        value = pz[holder_ref[s]]
        stage[s] = value
        fbuf[s, mz] = value
        return [
            remote(stage.at[s], fbuf.at[s, mz], z_send.at[2 + s, d - 1], z_recv.at[2 + s, d - 1], at_z(d))
            for d in range(1, depth)
        ]

    block_copies = {0: send_block(0)}

    finish(inverse_copies)
    for s in range(STEPS):
        invf[s, mx, my] = iz[holder_ref[s]]
    low, high = pl.ds(0, half), pl.ds(half, half)
    copies = []
    for d in range(1, side):
        src = invf.at[:, mx, my, :, low]
        copies.append(remote(src, src, i_send.at[0, d - 1], i_recv.at[0, d - 1], at_x(d)))
        src = invf.at[:, mx, my, :, high]
        copies.append(remote(src, src, i_send.at[1, d - 1], i_recv.at[1, d - 1], at_y(d)))
    finish(copies)
    copies = []
    for d in range(1, side):
        src = invf.at[:, :, my, :, low]
        copies.append(remote(src, src, i_send.at[2, d - 1], i_recv.at[2, d - 1], at_y(d)))
        src = invf.at[:, mx, :, :, high]
        copies.append(remote(src, src, i_send.at[3, d - 1], i_recv.at[3, d - 1], at_x(d)))
    finish(copies)

    def dot(a, b):
        return jnp.dot(a, b, preferred_element_type=F32)

    def dot_back(a, b):
        return lax.dot_general(a, b, (((1,), (1,)), ((), ())), preferred_element_type=F32)

    def three(product, a, b_high, b_low):
        a_high, a_low = a
        return product(a_high, b_high) + (product(a_high, b_low) + product(a_low, b_high))

    def prepare(s):
        finish(block_copies[s])
        slot = s % 2
        extra = out_ref.shape[1] - rows
        place = lax.broadcasted_iota(jnp.int32, (extra, half), 0) - share * chosen_ref[s]
        inside = (place >= 0) & (place < share)
        lane = lax.broadcasted_iota(jnp.int32, (extra, half), 1)
        for h in range(2):
            f_high, f_low = split(fbuf[s, :, :, h * half : (h + 1) * half].reshape(rows, half))
            hit = inside & (share * r + place == lane + h * half)
            wide[slot, h, :rows] = f_high
            wide_back[slot, h, :rows] = f_high
            wide_low[slot, h, :rows] = f_low
            wide[slot, h, rows:] = jnp.where(hit, -penalty, 0.0).astype(BF16)
            wide_back[slot, h, rows:] = jnp.where(hit, -1.0, 0.0).astype(BF16)
            wide_low[slot, h, rows:] = jnp.zeros((extra, half), BF16)
        i_high, i_low = split(invf[s].reshape(half, 2 * half))
        inv_high[slot] = i_high
        inv_low[slot] = i_low

    offsets = [side * side * sum(parts[:c]) for c in range(count)]
    live = {}

    def correlate(s, c):
        slot, size = s % 2, side * side * parts[c]
        x = split(out_ref[offsets[c] : offsets[c] + size, :])
        shape = (side, side, parts[c], half)
        cbuf[c][other] = three(dot, x, wide[slot, other], wide_low[slot, other]).reshape(shape)
        live[c] = [remote(cbuf[c].at[other], cother[c], c_send.at[0, c], c_recv.at[0, c], partner)]
        cbuf[c][core] = three(dot, x, wide[slot, core], wide_low[slot, core]).reshape(shape)

    def scatter_first(s, c):
        finish(live[c])
        cbuf[c][core] = cbuf[c][core] + cother[c][...]
        live[c] = []
        for d in range(1, side):
            src = cbuf[c].at[core, lax.rem(mx + d, side), :, :, pl.ds(0, quarter)]
            live[c].append(remote(src, rs1x[c].at[d - 1], t_send.at[0, c, d - 1], t_recv.at[0, c, d - 1], at_x(d)))
            src = cbuf[c].at[core, :, lax.rem(my + d, side), :, pl.ds(quarter, quarter)]
            live[c].append(remote(src, rs1y[c].at[d - 1], t_send.at[1, c, d - 1], t_recv.at[1, c, d - 1], at_y(d)))

    def scatter_second(s, c):
        finish(live[c])
        live[c] = []
        sum_x = cbuf[c][core, mx, :, :, :quarter]
        sum_y = cbuf[c][core, :, my, :, quarter:]
        for d in range(1, side):
            sum_x = sum_x + rs1x[c][d - 1]
            sum_y = sum_y + rs1y[c][d - 1]
        t1x[c][...] = sum_x
        t1y[c][...] = sum_y
        for d in range(1, side):
            src = t1x[c].at[lax.rem(my + d, side)]
            live[c].append(remote(src, rs2x[c].at[d - 1], t_send.at[2, c, d - 1], t_recv.at[2, c, d - 1], at_y(d)))
            src = t1y[c].at[lax.rem(mx + d, side)]
            live[c].append(remote(src, rs2y[c].at[d - 1], t_send.at[3, c, d - 1], t_recv.at[3, c, d - 1], at_x(d)))

    def target(s, c):
        finish(live[c])
        sum_x = t1x[c][my]
        sum_y = t1y[c][mx]
        for d in range(1, side):
            sum_x = sum_x + rs2x[c][d - 1]
            sum_y = sum_y + rs2y[c][d - 1]
        tfull[c][core, :, :quarter] = sum_x
        tfull[c][core, :, quarter:] = sum_y
        live[c] = [remote(tfull[c].at[core], tfull[c].at[core], c_send.at[1, c], c_recv.at[1, c], partner)]

    def solve(s, c):
        finish(live[c])
        slot = s % 2
        change = three(dot_back, split(tfull[c][0]), inv_high[slot, :, :half], inv_low[slot, :, :half])
        change += three(dot_back, split(tfull[c][1]), inv_high[slot, :, half:], inv_low[slot, :, half:])
        dfull[c][core, mx, my] = change * inv_rows
        live[c] = []
        for d in range(1, side):
            src = dfull[c].at[core, mx, my, :, pl.ds(0, quarter)]
            live[c].append(remote(src, src, t_send.at[4, c, d - 1], t_recv.at[4, c, d - 1], at_x(d)))
            src = dfull[c].at[core, mx, my, :, pl.ds(quarter, quarter)]
            live[c].append(remote(src, src, t_send.at[5, c, d - 1], t_recv.at[5, c, d - 1], at_y(d)))

    def gather_second(s, c):
        finish(live[c])
        live[c] = []
        for d in range(1, side):
            src = dfull[c].at[core, :, my, :, pl.ds(0, quarter)]
            live[c].append(remote(src, src, t_send.at[6, c, d - 1], t_recv.at[6, c, d - 1], at_y(d)))
            src = dfull[c].at[core, mx, :, :, pl.ds(quarter, quarter)]
            live[c].append(remote(src, src, t_send.at[7, c, d - 1], t_recv.at[7, c, d - 1], at_x(d)))

    def swap(s, c):
        finish(live[c])
        live[c] = [remote(dfull[c].at[core], dfull[c].at[core], c_send.at[2, c], c_recv.at[2, c], partner)]

    def update(s, c):
        finish(live[c])
        slot, size = s % 2, side * side * parts[c]
        gone = 0.0
        for h in range(2):
            d = split(dfull[c][h].reshape(size, half))
            gone = gone + three(dot_back, d, wide_back[slot, h], wide_low[slot, h])
        at = slice(offsets[c], offsets[c] + size)
        out_ref[at, :] = out_ref[at, :] - gone

    phases = [correlate, scatter_first, scatter_second, target, solve, gather_second, swap, update]
    lag = max(1, len(phases) // count)
    for tick in range(STEPS * len(phases) + lag * (count - 1)):
        for c in range(count):
            at = tick - lag * c
            if not 0 <= at < STEPS * len(phases):
                continue
            s, phase = divmod(at, len(phases))
            if c == 0 and phase == 0:
                prepare(s)
                if s + 1 < STEPS:
                    block_copies[s + 1] = send_block(s + 1)
            phases[phase](s, c)


def body(side, depth, features, inverses, weights, residual, order, owner):
    rows, classes = residual.shape
    width = features.shape[2]
    half, quarter = width // 2, width // 4
    share = weights.shape[1]
    chips = side * side
    parts = plan(classes // chips)
    r = lax.axis_index("rows")
    begin = lax.rem(r, 2) * half + lax.div(r, 2) * share
    inverse = lax.dynamic_slice_in_dim(inverses[0], begin, share, 0)
    stored = weights.reshape(weights.shape[0] * share, classes)
    state = jnp.concatenate([residual, stored], axis=0).T
    deep = state.shape[1]
    piece = rows // depth
    scratch = [
        pltpu.VMEM((depth, piece, width), F32),
        pltpu.VMEM((STEPS, piece, width), F32),
        pltpu.VMEM((STEPS, depth, piece, width), F32),
        pltpu.VMEM((depth, share, width), F32),
        pltpu.VMEM((STEPS, side, side, share, width), F32),
        pltpu.VMEM((2, 2, deep, half), BF16),
        pltpu.VMEM((2, 2, deep, half), BF16),
        pltpu.VMEM((2, 2, deep, half), BF16),
        pltpu.VMEM((2, half, width), BF16),
        pltpu.VMEM((2, half, width), BF16),
        pltpu.SemaphoreType.DMA((2 + STEPS, depth - 1)),
        pltpu.SemaphoreType.DMA((2 + STEPS, depth - 1)),
        pltpu.SemaphoreType.DMA((4, side - 1)),
        pltpu.SemaphoreType.DMA((4, side - 1)),
        pltpu.SemaphoreType.DMA((3, len(parts))),
        pltpu.SemaphoreType.DMA((3, len(parts))),
        pltpu.SemaphoreType.DMA((8, len(parts), side - 1)),
        pltpu.SemaphoreType.DMA((8, len(parts), side - 1)),
    ]
    for shape in (
        lambda p: (2, side, side, p, half),
        lambda p: (side, side, p, half),
        lambda p: (side - 1, side, p, quarter),
        lambda p: (side - 1, side, p, quarter),
        lambda p: (side, p, quarter),
        lambda p: (side, p, quarter),
        lambda p: (side - 1, p, quarter),
        lambda p: (side - 1, p, quarter),
        lambda p: (2, p, half),
        lambda p: (2, side, side, p, half),
    ):
        scratch += [pltpu.VMEM(shape(p), F32) for p in parts]
    vmem = pl.BlockSpec(memory_space=pltpu.VMEM)
    smem = pl.BlockSpec(memory_space=pltpu.SMEM)
    state = pl.pallas_call(
        functools.partial(kernel, side, depth, parts),
        out_shape=jax.ShapeDtypeStruct(state.shape, F32),
        in_specs=[smem, smem, vmem, vmem, vmem],
        out_specs=vmem,
        scratch_shapes=scratch,
        compiler_params=pltpu.CompilerParams(collective_id=0, has_side_effects=True, vmem_limit_bytes=56 << 20),
        cost_estimate=pl.CostEstimate(flops=14 * 10**9, bytes_accessed=8 * 10**6, transcendentals=0),
    )(order, owner[order], state, features[0], inverse)
    back = state.T
    return back[rows:].reshape(weights.shape), back[:rows]


def solution(mesh):
    side = {32: 4, 8: 2}[mesh.shape["rows"]]
    return jax.shard_map(
        functools.partial(body, side, mesh.shape["cls"]),
        mesh=mesh,
        in_specs=(
            P("cls", "rows", None),
            P("cls", None, None),
            P(None, "rows", "cls"),
            P("rows", "cls"),
            P(),
            P(),
        ),
        out_specs=(P(None, "rows", "cls"), P("rows", "cls")),
        check_vma=False,
    )
```

```python
import functools

import jax
import jax.numpy as jnp
from jax import lax
from jax.experimental import pallas as pl
from jax.experimental.pallas import tpu as pltpu
from jax.sharding import PartitionSpec as P

STEPS = 3
MESH = pl.DeviceIdType.MESH
F32 = jnp.float32
BF16 = jnp.bfloat16


def split(value):
    high = value.astype(BF16)
    return high, (value - high.astype(F32)).astype(BF16)


def plan(chip_rows):
    eighths = chip_rows // 8
    count = min(4, eighths)
    return tuple(8 * (eighths // count + (c < eighths % count)) for c in range(count))


PHASES = 8
PREPARE = 8
GATHER = 9


def schedule(parts, depth):
    total = sum(parts)
    works = [c / total for c in parts]
    compute = (4.5, 0.8, 0.5, 0.2, 1.5, 0.0, 0.0, 4.5)
    fixed = (0.1, 0.4, 0.4, 0.2, 0.5, 0.4, 0.1, 0.1)
    moves = ((0, 3.4), (1, 7.2), (1, 1.8), (0, 0.2), (1, 1.8), (1, 7.2), (0, 3.4), None)
    delay = (1.0, 2.5)
    free = [0.0, 0.0]
    now = 0.0
    ready = [0.0] * len(parts)
    place = [0] * len(parts)
    gather_ready, gather_place = 6.0, 0
    block_ready = [0.0] + [18.0 * s for s in range(1, STEPS)]
    prepared, done, solved = 0, [0] * STEPS, [0] * STEPS
    order = []
    while min(place) < STEPS * PHASES:
        options = []
        for c in range(len(parts)):
            if place[c] == STEPS * PHASES:
                continue
            s, phase = divmod(place[c], PHASES)
            if phase == 0 and prepared <= s:
                continue
            if phase == 4 and gather_place < 3 * s + 3:
                continue
            options.append((max(ready[c], now), place[c], phase, s, c))
        if prepared < STEPS and (prepared < 2 or done[prepared - 2] == len(parts)):
            if any(p == prepared * PHASES for p in place):
                options.append((max(block_ready[prepared], now), -1, PREPARE, prepared, 0))
        s, stage = divmod(gather_place, 3)
        if s < STEPS and (stage < 2 or s < 2 or solved[s - 2] == len(parts)) and max(place) >= (s - 1) * PHASES + 2:
            options.append((max(gather_ready, now), s * PHASES + 3, GATHER + stage, s, 0))
        start, _, kind, s, c = min(options)
        order.append((kind, s, c))
        now = start
        if kind == PREPARE:
            now += 1.0
            prepared += 1
        elif kind >= GATHER:
            now += 0.5
            if kind < GATHER + 2:
                free[1] = max(free[1], now) + (0.7, 2.6)[kind - GATHER]
                gather_ready = free[1] + delay[1]
            gather_place += 1
        else:
            now += compute[kind] * works[c] + fixed[kind]
            place[c] += 1
            ready[c] = now
            if moves[kind]:
                link, long = moves[kind]
                free[link] = max(free[link], now) + long * works[c]
                ready[c] = free[link] + delay[link]
            done[s] += kind == PHASES - 1
            solved[s] += kind == 4
    return order


def kernel(side, depth, parts, chosen_ref, owner_ref, f_ref, all_inverse, w_in, r_in, w_out, r_out, *scratch):
    count = len(parts)
    (i_ref, w_ref, r_ref, w_back, r_back, out_ref) = scratch[:6]
    (pz, stage, fbuf, iz, invf, wide, wide_low, wide_back, inv_high, inv_low) = scratch[6:16]
    (z_send, z_recv, i_send, i_recv, c_send, c_recv, t_send, t_recv, l_sem) = scratch[16:25]
    per_part = scratch[25:]
    cbuf, cother, rs1, t1x, t1y, rs2, tfull, dfull = (per_part[k * count : (k + 1) * count] for k in range(8))
    rows, width = f_ref.shape[1:]
    half = width // 2
    quarter = half // 2
    total_rows = rows * side * side * 2
    penalty = total_rows / 64.0
    inv_rows = 1.0 / total_rows
    share = i_ref.shape[0]
    blocks = w_in.shape[0]
    piece = rows // depth

    r = lax.axis_index("rows")
    mz = lax.axis_index("cls")
    core = lax.rem(r, 2)
    other = 1 - core
    my = lax.rem(lax.div(r, 2), side)
    mx = lax.div(r, 2 * side)

    def at_x(d):
        return ((lax.rem(mx + d, side) * side + my) * 2 + core, mz)

    def at_y(d):
        return ((mx * side + lax.rem(my + d, side)) * 2 + core, mz)

    def at_z(d):
        return (r, lax.rem(mz + d, depth))

    partner = ((mx * side + my) * 2 + other, mz)

    begin = pl.multiple_of(core * half + (mx * side + my) * share, share)
    load_inverse = pltpu.make_async_copy(all_inverse.at[0, pl.ds(begin, share)], i_ref, l_sem.at[0])
    load_inverse.start()
    load_r = pltpu.make_async_copy(r_in, r_ref, l_sem.at[1])
    load_r.start()
    load_w = pltpu.make_async_copy(w_in, w_ref, l_sem.at[2])
    load_w.start()

    barrier = pltpu.get_barrier_semaphore()
    peers = (
        [at_x(d) for d in range(1, side)]
        + [at_y(d) for d in range(1, side)]
        + [at_z(d) for d in range(1, depth)]
        + [partner]
    )
    for peer in peers:
        pl.semaphore_signal(barrier, inc=1, device_id=peer, device_id_type=MESH)
    pl.semaphore_wait(barrier, len(peers))

    def remote(src, dst, send, recv, device):
        copy = pltpu.make_async_remote_copy(
            src_ref=src, dst_ref=dst, send_sem=send, recv_sem=recv, device_id=device, device_id_type=MESH
        )
        copy.start()
        return copy

    def joint(ref, send, recv):
        return pltpu.make_async_remote_copy(
            src_ref=ref, dst_ref=ref, send_sem=send, recv_sem=recv, device_id=partner, device_id_type=MESH
        )

    for d in range(1, depth):
        to = lax.rem(mz + d, depth)
        src = f_ref.at[0, pl.ds(to * piece, piece)]
        remote(src, pz.at[mz], z_send.at[0], z_recv.at[0], at_z(d))
    pz[mz] = f_ref[0, pl.ds(mz * piece, piece)]

    def send_block(s):
        value = pz[owner_ref[chosen_ref[s]]]
        stage[s] = value
        fbuf[s, mz] = value
        for d in range(1, depth):
            remote(stage.at[s], fbuf.at[s, mz], z_send.at[2 + s], z_recv.at[2 + s], at_z(d))

    offsets = [side * side * sum(parts[:c]) for c in range(count)]
    def send_inverse():
        load_inverse.wait()
        for d in range(1, depth):
            remote(i_ref, iz.at[mz], z_send.at[1], z_recv.at[1], at_z(d))
        iz[mz] = i_ref[...]

    def turn_over(c):
        size = side * side * parts[c]
        at = slice(offsets[c], offsets[c] + size)
        out_ref[at, :rows] = r_ref[:, at].T
        out_ref[at, rows:] = w_ref[:, :, at].reshape(blocks * share, size).T

    others = pl.ds(0, depth - 1)
    joint(pz.at[others], z_send.at[0], z_recv.at[0]).wait()
    send_block(0)
    send_inverse()
    load_r.wait()
    load_w.wait()
    for c in range(count):
        turn_over(c)

    low, high = pl.ds(0, half), pl.ds(half, half)

    def inverse_first(s):
        if s == 0:
            joint(iz.at[others], z_send.at[1], z_recv.at[1]).wait()
        invf[s, mx, my] = iz[owner_ref[chosen_ref[s]]]
        for d in range(1, side):
            src = invf.at[s, mx, my, :, low]
            remote(src, src, i_send.at[s, 0], i_recv.at[s, 0], at_x(d))
            src = invf.at[s, mx, my, :, high]
            remote(src, src, i_send.at[s, 0], i_recv.at[s, 0], at_y(d))

    def inverse_second(s):
        joint(iz.at[pl.ds(0, side - 1)], i_send.at[s, 0], i_recv.at[s, 0]).wait()
        for d in range(1, side):
            src = invf.at[s, :, my, :, low]
            remote(src, src, i_send.at[s, 1], i_recv.at[s, 1], at_y(d))
            src = invf.at[s, mx, :, :, high]
            remote(src, src, i_send.at[s, 1], i_recv.at[s, 1], at_x(d))

    def inverse_third(s):
        joint(invf.at[s, pl.ds(0, side - 1)], i_send.at[s, 1], i_recv.at[s, 1]).wait()
        slot = s % 2
        i_high, i_low = split(invf[s].reshape(half, 2 * half))
        inv_high[slot] = i_high
        inv_low[slot] = i_low

    def dot(a, b):
        return jnp.dot(a, b, preferred_element_type=F32)

    def dot_back(a, b):
        return lax.dot_general(a, b, (((1,), (1,)), ((), ())), preferred_element_type=F32)

    def three(product, a, b_high, b_low):
        a_high, a_low = a
        return product(a_high, b_high) + (product(a_high, b_low) + product(a_low, b_high))

    def prepare(s):
        joint(fbuf.at[s, others], z_send.at[2 + s], z_recv.at[2 + s]).wait()
        if s + 1 < STEPS:
            send_block(s + 1)
        slot = s % 2
        extra = out_ref.shape[1] - rows
        place = lax.broadcasted_iota(jnp.int32, (extra, half), 0) - share * chosen_ref[s]
        inside = (place >= 0) & (place < share)
        lane = lax.broadcasted_iota(jnp.int32, (extra, half), 1)
        block = fbuf[s].reshape(rows, width)
        for h in range(2):
            f_high, f_low = split(block[:, h * half : (h + 1) * half])
            hit = inside & (share * r + place == lane + h * half)
            wide[slot, h, :rows] = f_high
            wide_back[slot, h, :rows] = f_high
            wide_low[slot, h, :rows] = f_low
            wide[slot, h, rows:] = jnp.where(hit, -penalty, 0.0).astype(BF16)
            wide_back[slot, h, rows:] = jnp.where(hit, -1.0, 0.0).astype(BF16)
            wide_low[slot, h, rows:] = jnp.zeros((extra, half), BF16)

    live = {}
    stores = []

    def correlate(s, c):
        slot, size = s % 2, side * side * parts[c]
        x = split(out_ref[offsets[c] : offsets[c] + size, :])
        shape = (side, side, parts[c], half)
        cbuf[c][other] = three(dot, x, wide[slot, other], wide_low[slot, other]).reshape(shape)
        live[c] = remote(cbuf[c].at[other], cother[c], c_send.at[0, c], c_recv.at[0, c], partner)
        cbuf[c][core] = three(dot, x, wide[slot, core], wide_low[slot, core]).reshape(shape)

    def scatter_first(s, c):
        live[c].wait()
        cbuf[c][core] = cbuf[c][core] + cother[c][...]
        for d in range(1, side):
            src = cbuf[c].at[core, lax.rem(mx + d, side), :, :, pl.ds(0, quarter)]
            remote(src, rs1[c].at[d - 1], t_send.at[0, c], t_recv.at[0, c], at_x(d))
            src = cbuf[c].at[core, :, lax.rem(my + d, side), :, pl.ds(quarter, quarter)]
            remote(src, rs1[c].at[side - 2 + d], t_send.at[0, c], t_recv.at[0, c], at_y(d))
        live[c] = joint(rs1[c], t_send.at[0, c], t_recv.at[0, c])

    def scatter_second(s, c):
        live[c].wait()
        sum_x = cbuf[c][core, mx, :, :, :quarter]
        sum_y = cbuf[c][core, :, my, :, quarter:]
        for d in range(1, side):
            sum_x = sum_x + rs1[c][d - 1]
            sum_y = sum_y + rs1[c][side - 2 + d]
        t1x[c][...] = sum_x
        t1y[c][...] = sum_y
        for d in range(1, side):
            src = t1x[c].at[lax.rem(my + d, side)]
            remote(src, rs2[c].at[d - 1], t_send.at[1, c], t_recv.at[1, c], at_y(d))
            src = t1y[c].at[lax.rem(mx + d, side)]
            remote(src, rs2[c].at[side - 2 + d], t_send.at[1, c], t_recv.at[1, c], at_x(d))
        live[c] = joint(rs2[c], t_send.at[1, c], t_recv.at[1, c])

    def target(s, c):
        live[c].wait()
        sum_x = t1x[c][my]
        sum_y = t1y[c][mx]
        for d in range(1, side):
            sum_x = sum_x + rs2[c][d - 1]
            sum_y = sum_y + rs2[c][side - 2 + d]
        tfull[c][core, :, :quarter] = sum_x
        tfull[c][core, :, quarter:] = sum_y
        live[c] = remote(tfull[c].at[core], tfull[c].at[core], c_send.at[1, c], c_recv.at[1, c], partner)

    def solve(s, c):
        live[c].wait()
        slot = s % 2
        change = three(dot_back, split(tfull[c][0]), inv_high[slot, :, :half], inv_low[slot, :, :half])
        change += three(dot_back, split(tfull[c][1]), inv_high[slot, :, half:], inv_low[slot, :, half:])
        dfull[c][core, mx, my] = change * inv_rows
        for d in range(1, side):
            src = dfull[c].at[core, mx, my, :, pl.ds(0, quarter)]
            remote(src, src, t_send.at[2, c], t_recv.at[2, c], at_x(d))
            src = dfull[c].at[core, mx, my, :, pl.ds(quarter, quarter)]
            remote(src, src, t_send.at[2, c], t_recv.at[2, c], at_y(d))
        live[c] = joint(rs2[c], t_send.at[2, c], t_recv.at[2, c])

    def gather_second(s, c):
        live[c].wait()
        for d in range(1, side):
            src = dfull[c].at[core, :, my, :, pl.ds(0, quarter)]
            remote(src, src, t_send.at[3, c], t_recv.at[3, c], at_y(d))
            src = dfull[c].at[core, mx, :, :, pl.ds(quarter, quarter)]
            remote(src, src, t_send.at[3, c], t_recv.at[3, c], at_x(d))
        live[c] = joint(rs1[c], t_send.at[3, c], t_recv.at[3, c])

    def swap(s, c):
        live[c].wait()
        live[c] = remote(dfull[c].at[core], dfull[c].at[core], c_send.at[2, c], c_recv.at[2, c], partner)

    def update(s, c):
        live[c].wait()
        slot, size = s % 2, side * side * parts[c]
        gone = 0.0
        for h in range(2):
            d = split(dfull[c][h].reshape(size, half))
            gone = gone + three(dot_back, d, wide_back[slot, h], wide_low[slot, h])
        at = slice(offsets[c], offsets[c] + size)
        if s + 1 < STEPS:
            out_ref[at, :] = out_ref[at, :] - gone
            return
        last = out_ref[at, :] - gone
        r_back[:, at] = last[:, :rows].T
        w_back[:, :, at] = last[:, rows:].T.reshape(blocks, share, size)
        for k, (src, dst) in enumerate(((r_back.at[:, at], r_out.at[:, at]), (w_back.at[:, :, at], w_out.at[:, :, at]))):
            copy = pltpu.make_async_copy(src, dst, l_sem.at[3 + 2 * c + k])
            copy.start()
            stores.append(copy)

    phases = [correlate, scatter_first, scatter_second, target, solve, gather_second, swap, update]
    gathers = (inverse_first, inverse_second, inverse_third)
    for kind, s, c in schedule(parts, depth):
        if kind == PREPARE:
            prepare(s)
        elif kind >= GATHER:
            gathers[kind - GATHER](s)
        else:
            phases[kind](s, c)
    for copy in stores:
        copy.wait()


def body(side, depth, features, inverses, weights, residual, order, owner):
    rows, classes = residual.shape
    width = features.shape[2]
    half, quarter = width // 2, width // 4
    share = weights.shape[1]
    chips = side * side
    parts = plan(classes // chips)
    deep = rows + weights.shape[0] * share
    piece = rows // depth
    scratch = [
        pltpu.VMEM((share, width), F32),
        pltpu.VMEM(weights.shape, F32),
        pltpu.VMEM(residual.shape, F32),
        pltpu.VMEM(weights.shape, F32),
        pltpu.VMEM(residual.shape, F32),
        pltpu.VMEM((classes, deep), F32),
        pltpu.VMEM((depth, piece, width), F32),
        pltpu.VMEM((STEPS, piece, width), F32),
        pltpu.VMEM((STEPS, depth, piece, width), F32),
        pltpu.VMEM((depth, share, width), F32),
        pltpu.VMEM((STEPS, side, side, share, width), F32),
        pltpu.VMEM((2, 2, deep, half), BF16),
        pltpu.VMEM((2, 2, deep, half), BF16),
        pltpu.VMEM((2, 2, deep, half), BF16),
        pltpu.VMEM((2, half, width), BF16),
        pltpu.VMEM((2, half, width), BF16),
        pltpu.SemaphoreType.DMA((2 + STEPS,)),
        pltpu.SemaphoreType.DMA((2 + STEPS,)),
        pltpu.SemaphoreType.DMA((STEPS, 2)),
        pltpu.SemaphoreType.DMA((STEPS, 2)),
        pltpu.SemaphoreType.DMA((3, len(parts))),
        pltpu.SemaphoreType.DMA((3, len(parts))),
        pltpu.SemaphoreType.DMA((4, len(parts))),
        pltpu.SemaphoreType.DMA((4, len(parts))),
        pltpu.SemaphoreType.DMA((3 + 2 * len(parts),)),
    ]
    for shape in (
        lambda p: (2, side, side, p, half),
        lambda p: (side, side, p, half),
        lambda p: (2 * (side - 1), side, p, quarter),
        lambda p: (side, p, quarter),
        lambda p: (side, p, quarter),
        lambda p: (2 * (side - 1), p, quarter),
        lambda p: (2, p, half),
        lambda p: (2, side, side, p, half),
    ):
        scratch += [pltpu.VMEM(shape(p), F32) for p in parts]
    vmem = pl.BlockSpec(memory_space=pltpu.VMEM)
    smem = pl.BlockSpec(memory_space=pltpu.SMEM)
    hbm = pl.BlockSpec(memory_space=pl.ANY)
    return pl.pallas_call(
        functools.partial(kernel, side, depth, parts),
        out_shape=(jax.ShapeDtypeStruct(weights.shape, F32), jax.ShapeDtypeStruct(residual.shape, F32)),
        in_specs=[smem, smem, vmem, hbm, hbm, hbm],
        out_specs=(hbm, hbm),
        scratch_shapes=scratch,
        compiler_params=pltpu.CompilerParams(collective_id=0, has_side_effects=True, vmem_limit_bytes=60 << 20),
        cost_estimate=pl.CostEstimate(flops=14 * 10**9, bytes_accessed=8 * 10**6, transcendentals=0),
    )(order, owner, features, inverses, weights, residual)


def solution(mesh):
    side = {32: 4, 8: 2}[mesh.shape["rows"]]
    return jax.shard_map(
        functools.partial(body, side, mesh.shape["cls"]),
        mesh=mesh,
        in_specs=(
            P("cls", "rows", None),
            P("cls", None, None),
            P(None, "rows", "cls"),
            P("rows", "cls"),
            P(),
            P(),
        ),
        out_specs=(P(None, "rows", "cls"), P("rows", "cls")),
        check_vma=False,
    )
```

```python
import functools

import jax
import jax.numpy as jnp
from jax import lax
from jax.experimental import pallas as pl
from jax.experimental.pallas import tpu as pltpu
from jax.sharding import PartitionSpec as P

STEPS = 3
MESH = pl.DeviceIdType.MESH
F32 = jnp.float32
BF16 = jnp.bfloat16


def split(value):
    high = value.astype(BF16)
    return high, (value - high.astype(F32)).astype(BF16)


def plan(chip_rows):
    eighths = chip_rows // 8
    count = min(4, eighths)
    return tuple(8 * (eighths // count + (c < eighths % count)) for c in range(count))


PHASES = 8
PREPARE = 8
GATHER = 9


def schedule(parts, depth):
    total = sum(parts)
    works = [c / total for c in parts]
    compute = (4.5, 0.8, 0.5, 0.2, 1.5, 0.0, 0.0, 4.5)
    fixed = (0.1, 0.4, 0.4, 0.2, 0.5, 0.4, 0.1, 0.1)
    moves = ((0, 3.4), (1, 7.2), (1, 1.8), (0, 0.2), (1, 1.8), (1, 7.2), (0, 3.4), None)
    delay = (1.0, 2.5)
    free = [0.0, 0.0]
    now = 0.0
    ready = [0.0] * len(parts)
    place = [0] * len(parts)
    gather_ready, gather_place = 6.0, 0
    block_ready = [0.0] + [18.0 * s for s in range(1, STEPS)]
    prepared, done, solved = 0, [0] * STEPS, [0] * STEPS
    order = []
    while min(place) < STEPS * PHASES:
        options = []
        for c in range(len(parts)):
            if place[c] == STEPS * PHASES:
                continue
            s, phase = divmod(place[c], PHASES)
            if phase == 0 and prepared <= s:
                continue
            if phase == 4 and gather_place < 3 * s + 3:
                continue
            start = max(ready[c], now)
            if phase in (1, 5):
                start = max(start, free[1])
            options.append((start, -place[c], phase, s, c))
        if prepared < STEPS and (prepared < 2 or done[prepared - 2] == len(parts)):
            if any(p == prepared * PHASES for p in place):
                options.append((max(block_ready[prepared], now), -1, PREPARE, prepared, 0))
        s, stage = divmod(gather_place, 3)
        if s < STEPS and (stage < 2 or s < 2 or solved[s - 2] == len(parts)) and max(place) >= (s - 1) * PHASES + 2:
            options.append((max(gather_ready, now), s * PHASES + 3, GATHER + stage, s, 0))
        start, _, kind, s, c = min(options)
        order.append((kind, s, c))
        now = start
        if kind == PREPARE:
            now += 1.0
            prepared += 1
        elif kind >= GATHER:
            now += 0.5
            if kind < GATHER + 2:
                free[1] = max(free[1], now) + (0.7, 2.6)[kind - GATHER]
                gather_ready = free[1] + delay[1]
            gather_place += 1
        else:
            now += compute[kind] * works[c] + fixed[kind]
            place[c] += 1
            ready[c] = now
            if moves[kind]:
                link, long = moves[kind]
                free[link] = max(free[link], now) + long * works[c]
                ready[c] = free[link] + delay[link]
            done[s] += kind == PHASES - 1
            solved[s] += kind == 4
    return order


def kernel(side, depth, parts, chosen_ref, owner_ref, f_ref, all_inverse, w_in, r_in, w_out, r_out, *scratch):
    count = len(parts)
    (i_ref, w_ref, r_ref, w_back, r_back, out_ref) = scratch[:6]
    (pz, stage, fbuf, iz, invf, wide, wide_low, wide_back, inv_high, inv_low) = scratch[6:16]
    (z_send, z_recv, i_send, i_recv, c_send, c_recv, t_send, t_recv, l_sem) = scratch[16:25]
    per_part = scratch[25:]
    cbuf, cother, rs1, t1x, t1y, rs2, tfull, dfull = (per_part[k * count : (k + 1) * count] for k in range(8))
    rows, width = f_ref.shape[1:]
    half = width // 2
    quarter = half // 2
    total_rows = rows * side * side * 2
    penalty = total_rows / 64.0
    inv_rows = 1.0 / total_rows
    share = i_ref.shape[0]
    blocks = w_in.shape[0]
    piece = rows // depth

    r = lax.axis_index("rows")
    mz = lax.axis_index("cls")
    core = lax.rem(r, 2)
    other = 1 - core
    my = lax.rem(lax.div(r, 2), side)
    mx = lax.div(r, 2 * side)

    def at_x(d):
        return ((lax.rem(mx + d, side) * side + my) * 2 + core, mz)

    def at_y(d):
        return ((mx * side + lax.rem(my + d, side)) * 2 + core, mz)

    def at_z(d):
        return (r, lax.rem(mz + d, depth))

    partner = ((mx * side + my) * 2 + other, mz)

    begin = pl.multiple_of(core * half + (mx * side + my) * share, share)
    load_inverse = pltpu.make_async_copy(all_inverse.at[0, pl.ds(begin, share)], i_ref, l_sem.at[0])
    load_inverse.start()
    load_r = pltpu.make_async_copy(r_in, r_ref, l_sem.at[1])
    load_r.start()
    load_w = pltpu.make_async_copy(w_in, w_ref, l_sem.at[2])
    load_w.start()

    barrier = pltpu.get_barrier_semaphore()
    peers = (
        [at_x(d) for d in range(1, side)]
        + [at_y(d) for d in range(1, side)]
        + [at_z(d) for d in range(1, depth)]
        + [partner]
    )
    for peer in peers:
        pl.semaphore_signal(barrier, inc=1, device_id=peer, device_id_type=MESH)
    pl.semaphore_wait(barrier, len(peers))

    def remote(src, dst, send, recv, device):
        copy = pltpu.make_async_remote_copy(
            src_ref=src, dst_ref=dst, send_sem=send, recv_sem=recv, device_id=device, device_id_type=MESH
        )
        copy.start()
        return copy

    def joint(ref, send, recv):
        return pltpu.make_async_remote_copy(
            src_ref=ref, dst_ref=ref, send_sem=send, recv_sem=recv, device_id=partner, device_id_type=MESH
        )

    for d in range(1, depth):
        to = lax.rem(mz + d, depth)
        src = f_ref.at[0, pl.ds(to * piece, piece)]
        remote(src, pz.at[mz], z_send.at[0], z_recv.at[0], at_z(d))
    pz[mz] = f_ref[0, pl.ds(mz * piece, piece)]

    def send_block(s):
        value = pz[owner_ref[chosen_ref[s]]]
        stage[s] = value
        fbuf[s, mz] = value
        for d in range(1, depth):
            remote(stage.at[s], fbuf.at[s, mz], z_send.at[2 + s], z_recv.at[2 + s], at_z(d))

    offsets = [side * side * sum(parts[:c]) for c in range(count)]
    def send_inverse():
        load_inverse.wait()
        for d in range(1, depth):
            remote(i_ref, iz.at[mz], z_send.at[1], z_recv.at[1], at_z(d))
        iz[mz] = i_ref[...]

    def turn_over(c):
        size = side * side * parts[c]
        at = slice(offsets[c], offsets[c] + size)
        out_ref[at, :rows] = r_ref[:, at].T
        out_ref[at, rows:] = w_ref[:, :, at].reshape(blocks * share, size).T

    others = pl.ds(0, depth - 1)
    joint(pz.at[others], z_send.at[0], z_recv.at[0]).wait()
    send_block(0)
    send_inverse()
    load_r.wait()
    load_w.wait()
    for c in range(count):
        turn_over(c)

    low, high = pl.ds(0, half), pl.ds(half, half)

    def inverse_first(s):
        if s == 0:
            joint(iz.at[others], z_send.at[1], z_recv.at[1]).wait()
        invf[s, mx, my] = iz[owner_ref[chosen_ref[s]]]
        for d in range(1, side):
            src = invf.at[s, mx, my, :, low]
            remote(src, src, i_send.at[s, 0], i_recv.at[s, 0], at_x(d))
            src = invf.at[s, mx, my, :, high]
            remote(src, src, i_send.at[s, 0], i_recv.at[s, 0], at_y(d))

    def inverse_second(s):
        joint(iz.at[pl.ds(0, side - 1)], i_send.at[s, 0], i_recv.at[s, 0]).wait()
        for d in range(1, side):
            src = invf.at[s, :, my, :, low]
            remote(src, src, i_send.at[s, 1], i_recv.at[s, 1], at_y(d))
            src = invf.at[s, mx, :, :, high]
            remote(src, src, i_send.at[s, 1], i_recv.at[s, 1], at_x(d))

    def inverse_third(s):
        joint(invf.at[s, pl.ds(0, side - 1)], i_send.at[s, 1], i_recv.at[s, 1]).wait()
        slot = s % 2
        i_high, i_low = split(invf[s].reshape(half, 2 * half))
        inv_high[slot] = i_high
        inv_low[slot] = i_low

    def dot(a, b):
        return jnp.dot(a, b, preferred_element_type=F32)

    def dot_back(a, b):
        return lax.dot_general(a, b, (((1,), (1,)), ((), ())), preferred_element_type=F32)

    def three(product, a, b_high, b_low):
        a_high, a_low = a
        return product(a_high, b_high) + (product(a_high, b_low) + product(a_low, b_high))

    def prepare(s):
        joint(fbuf.at[s, others], z_send.at[2 + s], z_recv.at[2 + s]).wait()
        if s + 1 < STEPS:
            send_block(s + 1)
        slot = s % 2
        extra = out_ref.shape[1] - rows
        place = lax.broadcasted_iota(jnp.int32, (extra, half), 0) - share * chosen_ref[s]
        inside = (place >= 0) & (place < share)
        lane = lax.broadcasted_iota(jnp.int32, (extra, half), 1)
        block = fbuf[s].reshape(rows, width)
        for h in range(2):
            f_high, f_low = split(block[:, h * half : (h + 1) * half])
            hit = inside & (share * r + place == lane + h * half)
            wide[slot, h, :rows] = f_high
            wide_back[slot, h, :rows] = f_high
            wide_low[slot, h, :rows] = f_low
            wide[slot, h, rows:] = jnp.where(hit, -penalty, 0.0).astype(BF16)
            wide_back[slot, h, rows:] = jnp.where(hit, -1.0, 0.0).astype(BF16)
            wide_low[slot, h, rows:] = jnp.zeros((extra, half), BF16)

    live = {}
    stores = []

    def correlate(s, c):
        slot, size = s % 2, side * side * parts[c]
        x = split(out_ref[offsets[c] : offsets[c] + size, :])
        shape = (side, side, parts[c], half)
        cbuf[c][other] = three(dot, x, wide[slot, other], wide_low[slot, other]).reshape(shape)
        live[c] = remote(cbuf[c].at[other], cother[c], c_send.at[0, c], c_recv.at[0, c], partner)
        cbuf[c][core] = three(dot, x, wide[slot, core], wide_low[slot, core]).reshape(shape)

    def scatter_first(s, c):
        live[c].wait()
        cbuf[c][core] = cbuf[c][core] + cother[c][...]
        for d in range(1, side):
            src = cbuf[c].at[core, lax.rem(mx + d, side), :, :, pl.ds(0, quarter)]
            remote(src, rs1[c].at[d - 1], t_send.at[0, c], t_recv.at[0, c], at_x(d))
            src = cbuf[c].at[core, :, lax.rem(my + d, side), :, pl.ds(quarter, quarter)]
            remote(src, rs1[c].at[side - 2 + d], t_send.at[0, c], t_recv.at[0, c], at_y(d))
        live[c] = joint(rs1[c], t_send.at[0, c], t_recv.at[0, c])

    def scatter_second(s, c):
        live[c].wait()
        sum_x = cbuf[c][core, mx, :, :, :quarter]
        sum_y = cbuf[c][core, :, my, :, quarter:]
        for d in range(1, side):
            sum_x = sum_x + rs1[c][d - 1]
            sum_y = sum_y + rs1[c][side - 2 + d]
        t1x[c][...] = sum_x
        t1y[c][...] = sum_y
        for d in range(1, side):
            src = t1x[c].at[lax.rem(my + d, side)]
            remote(src, rs2[c].at[d - 1], t_send.at[1, c], t_recv.at[1, c], at_y(d))
            src = t1y[c].at[lax.rem(mx + d, side)]
            remote(src, rs2[c].at[side - 2 + d], t_send.at[1, c], t_recv.at[1, c], at_x(d))
        live[c] = joint(rs2[c], t_send.at[1, c], t_recv.at[1, c])

    def target(s, c):
        live[c].wait()
        sum_x = t1x[c][my]
        sum_y = t1y[c][mx]
        for d in range(1, side):
            sum_x = sum_x + rs2[c][d - 1]
            sum_y = sum_y + rs2[c][side - 2 + d]
        tfull[c][core, :, :quarter] = sum_x
        tfull[c][core, :, quarter:] = sum_y
        live[c] = remote(tfull[c].at[core], tfull[c].at[core], c_send.at[1, c], c_recv.at[1, c], partner)

    def solve(s, c):
        live[c].wait()
        slot = s % 2
        change = three(dot_back, split(tfull[c][0]), inv_high[slot, :, :half], inv_low[slot, :, :half])
        change += three(dot_back, split(tfull[c][1]), inv_high[slot, :, half:], inv_low[slot, :, half:])
        dfull[c][core, mx, my] = change * inv_rows
        for d in range(1, side):
            src = dfull[c].at[core, mx, my, :, pl.ds(0, quarter)]
            remote(src, src, t_send.at[2, c], t_recv.at[2, c], at_x(d))
            src = dfull[c].at[core, mx, my, :, pl.ds(quarter, quarter)]
            remote(src, src, t_send.at[2, c], t_recv.at[2, c], at_y(d))
        live[c] = joint(rs2[c], t_send.at[2, c], t_recv.at[2, c])

    def gather_second(s, c):
        live[c].wait()
        for d in range(1, side):
            src = dfull[c].at[core, :, my, :, pl.ds(0, quarter)]
            remote(src, src, t_send.at[3, c], t_recv.at[3, c], at_y(d))
            src = dfull[c].at[core, mx, :, :, pl.ds(quarter, quarter)]
            remote(src, src, t_send.at[3, c], t_recv.at[3, c], at_x(d))
        live[c] = joint(rs1[c], t_send.at[3, c], t_recv.at[3, c])

    def swap(s, c):
        live[c].wait()
        live[c] = remote(dfull[c].at[core], dfull[c].at[core], c_send.at[2, c], c_recv.at[2, c], partner)

    def update(s, c):
        live[c].wait()
        slot, size = s % 2, side * side * parts[c]
        gone = 0.0
        for h in range(2):
            d = split(dfull[c][h].reshape(size, half))
            gone = gone + three(dot_back, d, wide_back[slot, h], wide_low[slot, h])
        at = slice(offsets[c], offsets[c] + size)
        if s + 1 < STEPS:
            out_ref[at, :] = out_ref[at, :] - gone
            return
        last = out_ref[at, :] - gone
        r_back[:, at] = last[:, :rows].T
        w_back[:, :, at] = last[:, rows:].T.reshape(blocks, share, size)
        for k, (src, dst) in enumerate(((r_back.at[:, at], r_out.at[:, at]), (w_back.at[:, :, at], w_out.at[:, :, at]))):
            copy = pltpu.make_async_copy(src, dst, l_sem.at[3 + 2 * c + k])
            copy.start()
            stores.append(copy)

    phases = [correlate, scatter_first, scatter_second, target, solve, gather_second, swap, update]
    gathers = (inverse_first, inverse_second, inverse_third)
    for kind, s, c in schedule(parts, depth):
        if kind == PREPARE:
            prepare(s)
        elif kind >= GATHER:
            gathers[kind - GATHER](s)
        else:
            phases[kind](s, c)
    for copy in stores:
        copy.wait()


def body(side, depth, features, inverses, weights, residual, order, owner):
    rows, classes = residual.shape
    width = features.shape[2]
    half, quarter = width // 2, width // 4
    share = weights.shape[1]
    chips = side * side
    parts = plan(classes // chips)
    deep = rows + weights.shape[0] * share
    piece = rows // depth
    scratch = [
        pltpu.VMEM((share, width), F32),
        pltpu.VMEM(weights.shape, F32),
        pltpu.VMEM(residual.shape, F32),
        pltpu.VMEM(weights.shape, F32),
        pltpu.VMEM(residual.shape, F32),
        pltpu.VMEM((classes, deep), F32),
        pltpu.VMEM((depth, piece, width), F32),
        pltpu.VMEM((STEPS, piece, width), F32),
        pltpu.VMEM((STEPS, depth, piece, width), F32),
        pltpu.VMEM((depth, share, width), F32),
        pltpu.VMEM((STEPS, side, side, share, width), F32),
        pltpu.VMEM((2, 2, deep, half), BF16),
        pltpu.VMEM((2, 2, deep, half), BF16),
        pltpu.VMEM((2, 2, deep, half), BF16),
        pltpu.VMEM((2, half, width), BF16),
        pltpu.VMEM((2, half, width), BF16),
        pltpu.SemaphoreType.DMA((2 + STEPS,)),
        pltpu.SemaphoreType.DMA((2 + STEPS,)),
        pltpu.SemaphoreType.DMA((STEPS, 2)),
        pltpu.SemaphoreType.DMA((STEPS, 2)),
        pltpu.SemaphoreType.DMA((3, len(parts))),
        pltpu.SemaphoreType.DMA((3, len(parts))),
        pltpu.SemaphoreType.DMA((4, len(parts))),
        pltpu.SemaphoreType.DMA((4, len(parts))),
        pltpu.SemaphoreType.DMA((3 + 2 * len(parts),)),
    ]
    for shape in (
        lambda p: (2, side, side, p, half),
        lambda p: (side, side, p, half),
        lambda p: (2 * (side - 1), side, p, quarter),
        lambda p: (side, p, quarter),
        lambda p: (side, p, quarter),
        lambda p: (2 * (side - 1), p, quarter),
        lambda p: (2, p, half),
        lambda p: (2, side, side, p, half),
    ):
        scratch += [pltpu.VMEM(shape(p), F32) for p in parts]
    vmem = pl.BlockSpec(memory_space=pltpu.VMEM)
    smem = pl.BlockSpec(memory_space=pltpu.SMEM)
    hbm = pl.BlockSpec(memory_space=pl.ANY)
    return pl.pallas_call(
        functools.partial(kernel, side, depth, parts),
        out_shape=(jax.ShapeDtypeStruct(weights.shape, F32), jax.ShapeDtypeStruct(residual.shape, F32)),
        in_specs=[smem, smem, vmem, hbm, hbm, hbm],
        out_specs=(hbm, hbm),
        scratch_shapes=scratch,
        compiler_params=pltpu.CompilerParams(collective_id=0, has_side_effects=True, vmem_limit_bytes=60 << 20),
        cost_estimate=pl.CostEstimate(flops=14 * 10**9, bytes_accessed=8 * 10**6, transcendentals=0),
    )(order, owner, features, inverses, weights, residual)


def solution(mesh):
    side = {32: 4, 8: 2}[mesh.shape["rows"]]
    return jax.shard_map(
        functools.partial(body, side, mesh.shape["cls"]),
        mesh=mesh,
        in_specs=(
            P("cls", "rows", None),
            P("cls", None, None),
            P(None, "rows", "cls"),
            P("rows", "cls"),
            P(),
            P(),
        ),
        out_specs=(P(None, "rows", "cls"), P("rows", "cls")),
        check_vma=False,
    )
```

```python
import functools

import jax
import jax.numpy as jnp
from jax import lax
from jax.experimental import pallas as pl
from jax.experimental.pallas import tpu as pltpu
from jax.sharding import PartitionSpec as P

STEPS = 3
MESH = pl.DeviceIdType.MESH
F32 = jnp.float32
BF16 = jnp.bfloat16


def split(value):
    high = value.astype(BF16)
    return high, (value - high.astype(F32)).astype(BF16)


def plan(chip_rows):
    eighths = chip_rows // 8
    count = min(4, eighths)
    return tuple(8 * (eighths // count + (c < eighths % count)) for c in range(count))


PHASES = 8
PREPARE = 8


def schedule(parts, depth):
    total = sum(parts)
    works = [c / total for c in parts]
    compute = (4.5, 0.8, 0.5, 0.2, 1.5, 0.0, 0.0, 4.5)
    fixed = (0.1, 0.4, 0.4, 0.2, 0.5, 0.4, 0.1, 0.1)
    moves = ((0, 3.4), (1, 7.2), (1, 1.8), (0, 0.2), (1, 1.8), (1, 7.2), (0, 3.4), None)
    delay = (1.0, 2.5)
    free = [0.0, 0.0]
    now = 0.0
    ready = [0.0] * len(parts)
    place = [0] * len(parts)
    block_ready = [0.0] + [22.0 * s for s in range(1, STEPS)]
    prepared, done = 0, [0] * STEPS
    order = []
    while min(place) < STEPS * PHASES:
        options = []
        for c in range(len(parts)):
            if place[c] == STEPS * PHASES:
                continue
            s, phase = divmod(place[c], PHASES)
            if phase == 0 and prepared <= s:
                continue
            options.append((max(ready[c], now), place[c], phase, s, c))
        if prepared < STEPS and (prepared < 2 or done[prepared - 2] == len(parts)):
            options.append((max(block_ready[prepared], now), -1, PREPARE, prepared, 0))
        start, _, kind, s, c = min(options)
        order.append((kind, s, c))
        now = start
        if kind == PREPARE:
            now += 1.0
            prepared += 1
        else:
            now += compute[kind] * works[c] + fixed[kind]
            place[c] += 1
            ready[c] = now
            if moves[kind]:
                link, long = moves[kind]
                free[link] = max(free[link], now) + long * works[c]
                ready[c] = free[link] + delay[link]
            done[s] += kind == PHASES - 1
    return order


def kernel(side, depth, parts, chosen_ref, owner_ref, f_ref, all_inverse, w_in, r_in, w_out, r_out, *scratch):
    count = len(parts)
    (i_ref, w_ref, r_ref, w_back, r_back, out_ref) = scratch[:6]
    (pz, stage, fbuf, iz, invf, wide, wide_low, wide_back, inv_high, inv_low) = scratch[6:16]
    (z_send, z_recv, i_send, i_recv, c_send, c_recv, t_send, t_recv, l_sem) = scratch[16:25]
    per_part = scratch[25:]
    cbuf, cother, rs1, t1x, t1y, rs2, tfull, dfull = (per_part[k * count : (k + 1) * count] for k in range(8))
    rows, width = f_ref.shape[1:]
    half = width // 2
    quarter = half // 2
    total_rows = rows * side * side * 2
    penalty = total_rows / 64.0
    inv_rows = 1.0 / total_rows
    share = i_ref.shape[0]
    blocks = w_in.shape[0]
    piece = rows // depth

    r = lax.axis_index("rows")
    mz = lax.axis_index("cls")
    core = lax.rem(r, 2)
    other = 1 - core
    my = lax.rem(lax.div(r, 2), side)
    mx = lax.div(r, 2 * side)

    def at_x(d):
        return ((lax.rem(mx + d, side) * side + my) * 2 + core, mz)

    def at_y(d):
        return ((mx * side + lax.rem(my + d, side)) * 2 + core, mz)

    def at_z(d):
        return (r, lax.rem(mz + d, depth))

    partner = ((mx * side + my) * 2 + other, mz)

    begin = pl.multiple_of(core * half + (mx * side + my) * share, share)
    load_inverse = pltpu.make_async_copy(all_inverse.at[0, pl.ds(begin, share)], i_ref, l_sem.at[0])
    load_inverse.start()
    load_r = pltpu.make_async_copy(r_in, r_ref, l_sem.at[1])
    load_r.start()
    load_w = pltpu.make_async_copy(w_in, w_ref, l_sem.at[2])
    load_w.start()

    barrier = pltpu.get_barrier_semaphore()
    peers = (
        [at_x(d) for d in range(1, side)]
        + [at_y(d) for d in range(1, side)]
        + [at_z(d) for d in range(1, depth)]
        + [partner]
    )
    for peer in peers:
        pl.semaphore_signal(barrier, inc=1, device_id=peer, device_id_type=MESH)
    pl.semaphore_wait(barrier, len(peers))

    def remote(src, dst, send, recv, device):
        copy = pltpu.make_async_remote_copy(
            src_ref=src, dst_ref=dst, send_sem=send, recv_sem=recv, device_id=device, device_id_type=MESH
        )
        copy.start()
        return copy

    def joint(ref, send, recv):
        return pltpu.make_async_remote_copy(
            src_ref=ref, dst_ref=ref, send_sem=send, recv_sem=recv, device_id=partner, device_id_type=MESH
        )

    for d in range(1, depth):
        to = lax.rem(mz + d, depth)
        src = f_ref.at[0, pl.ds(to * piece, piece)]
        remote(src, pz.at[mz], z_send.at[0], z_recv.at[0], at_z(d))
    pz[mz] = f_ref[0, pl.ds(mz * piece, piece)]

    def send_block(s):
        value = pz[owner_ref[chosen_ref[s]]]
        stage[s] = value
        fbuf[s, mz] = value
        for d in range(1, depth):
            remote(stage.at[s], fbuf.at[s, mz], z_send.at[2 + s], z_recv.at[2 + s], at_z(d))

    offsets = [side * side * sum(parts[:c]) for c in range(count)]
    def send_inverse():
        load_inverse.wait()
        for d in range(1, depth):
            remote(i_ref, iz.at[mz], z_send.at[1], z_recv.at[1], at_z(d))
        iz[mz] = i_ref[...]

    def turn_over(c):
        size = side * side * parts[c]
        at = slice(offsets[c], offsets[c] + size)
        out_ref[at, :rows] = r_ref[:, at].T
        out_ref[at, rows:] = w_ref[:, :, at].reshape(blocks * share, size).T

    others = pl.ds(0, depth - 1)
    joint(pz.at[others], z_send.at[0], z_recv.at[0]).wait()
    send_block(0)
    send_inverse()
    load_r.wait()
    load_w.wait()
    for c in range(count):
        turn_over(c)

    low, high = pl.ds(0, half), pl.ds(half, half)

    def inverse_first(s):
        if s == 0:
            joint(iz.at[others], z_send.at[1], z_recv.at[1]).wait()
        invf[s, mx, my] = iz[owner_ref[chosen_ref[s]]]
        for d in range(1, side):
            src = invf.at[s, mx, my, :, low]
            remote(src, src, i_send.at[s, 0], i_recv.at[s, 0], at_x(d))
            src = invf.at[s, mx, my, :, high]
            remote(src, src, i_send.at[s, 0], i_recv.at[s, 0], at_y(d))

    def inverse_second(s):
        joint(iz.at[pl.ds(0, side - 1)], i_send.at[s, 0], i_recv.at[s, 0]).wait()
        for d in range(1, side):
            src = invf.at[s, :, my, :, low]
            remote(src, src, i_send.at[s, 1], i_recv.at[s, 1], at_y(d))
            src = invf.at[s, mx, :, :, high]
            remote(src, src, i_send.at[s, 1], i_recv.at[s, 1], at_x(d))

    def inverse_third(s):
        joint(invf.at[s, pl.ds(0, side - 1)], i_send.at[s, 1], i_recv.at[s, 1]).wait()
        i_high, i_low = split(invf[s].reshape(half, 2 * half))
        inv_high[s] = i_high
        inv_low[s] = i_low

    for gather in (inverse_first, inverse_second, inverse_third):
        for s in range(STEPS):
            gather(s)

    def dot(a, b):
        return jnp.dot(a, b, preferred_element_type=F32)

    def dot_back(a, b):
        return lax.dot_general(a, b, (((1,), (1,)), ((), ())), preferred_element_type=F32)

    def three(product, a, b_high, b_low):
        a_high, a_low = a
        return product(a_high, b_high) + (product(a_high, b_low) + product(a_low, b_high))

    def prepare(s):
        joint(fbuf.at[s, others], z_send.at[2 + s], z_recv.at[2 + s]).wait()
        if s + 1 < STEPS:
            send_block(s + 1)
        slot = s % 2
        extra = out_ref.shape[1] - rows
        place = lax.broadcasted_iota(jnp.int32, (extra, half), 0) - share * chosen_ref[s]
        inside = (place >= 0) & (place < share)
        lane = lax.broadcasted_iota(jnp.int32, (extra, half), 1)
        block = fbuf[s].reshape(rows, width)
        for h in range(2):
            f_high, f_low = split(block[:, h * half : (h + 1) * half])
            hit = inside & (share * r + place == lane + h * half)
            wide[slot, h, :rows] = f_high
            wide_back[slot, h, :rows] = f_high
            wide_low[slot, h, :rows] = f_low
            wide[slot, h, rows:] = jnp.where(hit, -penalty, 0.0).astype(BF16)
            wide_back[slot, h, rows:] = jnp.where(hit, -1.0, 0.0).astype(BF16)
            wide_low[slot, h, rows:] = jnp.zeros((extra, half), BF16)

    live = {}
    stores = []

    def correlate(s, c):
        slot, size = s % 2, side * side * parts[c]
        x = split(out_ref[offsets[c] : offsets[c] + size, :])
        shape = (side, side, parts[c], half)
        cbuf[c][other] = three(dot, x, wide[slot, other], wide_low[slot, other]).reshape(shape)
        live[c] = remote(cbuf[c].at[other], cother[c], c_send.at[0, c], c_recv.at[0, c], partner)
        cbuf[c][core] = three(dot, x, wide[slot, core], wide_low[slot, core]).reshape(shape)

    def scatter_first(s, c):
        live[c].wait()
        cbuf[c][core] = cbuf[c][core] + cother[c][...]
        for d in range(1, side):
            src = cbuf[c].at[core, lax.rem(mx + d, side), :, :, pl.ds(0, quarter)]
            remote(src, rs1[c].at[d - 1], t_send.at[0, c], t_recv.at[0, c], at_x(d))
            src = cbuf[c].at[core, :, lax.rem(my + d, side), :, pl.ds(quarter, quarter)]
            remote(src, rs1[c].at[side - 2 + d], t_send.at[0, c], t_recv.at[0, c], at_y(d))
        live[c] = joint(rs1[c], t_send.at[0, c], t_recv.at[0, c])

    def scatter_second(s, c):
        live[c].wait()
        sum_x = cbuf[c][core, mx, :, :, :quarter]
        sum_y = cbuf[c][core, :, my, :, quarter:]
        for d in range(1, side):
            sum_x = sum_x + rs1[c][d - 1]
            sum_y = sum_y + rs1[c][side - 2 + d]
        t1x[c][...] = sum_x
        t1y[c][...] = sum_y
        for d in range(1, side):
            src = t1x[c].at[lax.rem(my + d, side)]
            remote(src, rs2[c].at[d - 1], t_send.at[1, c], t_recv.at[1, c], at_y(d))
            src = t1y[c].at[lax.rem(mx + d, side)]
            remote(src, rs2[c].at[side - 2 + d], t_send.at[1, c], t_recv.at[1, c], at_x(d))
        live[c] = joint(rs2[c], t_send.at[1, c], t_recv.at[1, c])

    def target(s, c):
        live[c].wait()
        sum_x = t1x[c][my]
        sum_y = t1y[c][mx]
        for d in range(1, side):
            sum_x = sum_x + rs2[c][d - 1]
            sum_y = sum_y + rs2[c][side - 2 + d]
        tfull[c][core, :, :quarter] = sum_x
        tfull[c][core, :, quarter:] = sum_y
        live[c] = remote(tfull[c].at[core], tfull[c].at[core], c_send.at[1, c], c_recv.at[1, c], partner)

    def solve(s, c):
        live[c].wait()
        change = three(dot_back, split(tfull[c][0]), inv_high[s, :, :half], inv_low[s, :, :half])
        change += three(dot_back, split(tfull[c][1]), inv_high[s, :, half:], inv_low[s, :, half:])
        dfull[c][core, mx, my] = change * inv_rows
        for d in range(1, side):
            src = dfull[c].at[core, mx, my, :, pl.ds(0, quarter)]
            remote(src, src, t_send.at[2, c], t_recv.at[2, c], at_x(d))
            src = dfull[c].at[core, mx, my, :, pl.ds(quarter, quarter)]
            remote(src, src, t_send.at[2, c], t_recv.at[2, c], at_y(d))
        live[c] = joint(rs2[c], t_send.at[2, c], t_recv.at[2, c])

    def gather_second(s, c):
        live[c].wait()
        for d in range(1, side):
            src = dfull[c].at[core, :, my, :, pl.ds(0, quarter)]
            remote(src, src, t_send.at[3, c], t_recv.at[3, c], at_y(d))
            src = dfull[c].at[core, mx, :, :, pl.ds(quarter, quarter)]
            remote(src, src, t_send.at[3, c], t_recv.at[3, c], at_x(d))
        live[c] = joint(rs1[c], t_send.at[3, c], t_recv.at[3, c])

    def swap(s, c):
        live[c].wait()
        live[c] = remote(dfull[c].at[core], dfull[c].at[core], c_send.at[2, c], c_recv.at[2, c], partner)

    def update(s, c):
        live[c].wait()
        slot, size = s % 2, side * side * parts[c]
        gone = 0.0
        for h in range(2):
            d = split(dfull[c][h].reshape(size, half))
            gone = gone + three(dot_back, d, wide_back[slot, h], wide_low[slot, h])
        at = slice(offsets[c], offsets[c] + size)
        if s + 1 < STEPS:
            out_ref[at, :] = out_ref[at, :] - gone
            return
        last = out_ref[at, :] - gone
        r_back[:, at] = last[:, :rows].T
        w_back[:, :, at] = last[:, rows:].T.reshape(blocks, share, size)
        for k, (src, dst) in enumerate(((r_back.at[:, at], r_out.at[:, at]), (w_back.at[:, :, at], w_out.at[:, :, at]))):
            copy = pltpu.make_async_copy(src, dst, l_sem.at[3 + 2 * c + k])
            copy.start()
            stores.append(copy)

    phases = [correlate, scatter_first, scatter_second, target, solve, gather_second, swap, update]
    for kind, s, c in schedule(parts, depth):
        if kind == PREPARE:
            prepare(s)
        else:
            phases[kind](s, c)
    for copy in stores:
        copy.wait()


def body(side, depth, features, inverses, weights, residual, order, owner):
    rows, classes = residual.shape
    width = features.shape[2]
    half, quarter = width // 2, width // 4
    share = weights.shape[1]
    chips = side * side
    parts = plan(classes // chips)
    deep = rows + weights.shape[0] * share
    piece = rows // depth
    scratch = [
        pltpu.VMEM((share, width), F32),
        pltpu.VMEM(weights.shape, F32),
        pltpu.VMEM(residual.shape, F32),
        pltpu.VMEM(weights.shape, F32),
        pltpu.VMEM(residual.shape, F32),
        pltpu.VMEM((classes, deep), F32),
        pltpu.VMEM((depth, piece, width), F32),
        pltpu.VMEM((STEPS, piece, width), F32),
        pltpu.VMEM((STEPS, depth, piece, width), F32),
        pltpu.VMEM((depth, share, width), F32),
        pltpu.VMEM((STEPS, side, side, share, width), F32),
        pltpu.VMEM((2, 2, deep, half), BF16),
        pltpu.VMEM((2, 2, deep, half), BF16),
        pltpu.VMEM((2, 2, deep, half), BF16),
        pltpu.VMEM((STEPS, half, width), BF16),
        pltpu.VMEM((STEPS, half, width), BF16),
        pltpu.SemaphoreType.DMA((2 + STEPS,)),
        pltpu.SemaphoreType.DMA((2 + STEPS,)),
        pltpu.SemaphoreType.DMA((STEPS, 2)),
        pltpu.SemaphoreType.DMA((STEPS, 2)),
        pltpu.SemaphoreType.DMA((3, len(parts))),
        pltpu.SemaphoreType.DMA((3, len(parts))),
        pltpu.SemaphoreType.DMA((4, len(parts))),
        pltpu.SemaphoreType.DMA((4, len(parts))),
        pltpu.SemaphoreType.DMA((3 + 2 * len(parts),)),
    ]
    for shape in (
        lambda p: (2, side, side, p, half),
        lambda p: (side, side, p, half),
        lambda p: (2 * (side - 1), side, p, quarter),
        lambda p: (side, p, quarter),
        lambda p: (side, p, quarter),
        lambda p: (2 * (side - 1), p, quarter),
        lambda p: (2, p, half),
        lambda p: (2, side, side, p, half),
    ):
        scratch += [pltpu.VMEM(shape(p), F32) for p in parts]
    vmem = pl.BlockSpec(memory_space=pltpu.VMEM)
    smem = pl.BlockSpec(memory_space=pltpu.SMEM)
    hbm = pl.BlockSpec(memory_space=pl.ANY)
    return pl.pallas_call(
        functools.partial(kernel, side, depth, parts),
        out_shape=(jax.ShapeDtypeStruct(weights.shape, F32), jax.ShapeDtypeStruct(residual.shape, F32)),
        in_specs=[smem, smem, vmem, hbm, hbm, hbm],
        out_specs=(hbm, hbm),
        scratch_shapes=scratch,
        compiler_params=pltpu.CompilerParams(collective_id=0, has_side_effects=True, vmem_limit_bytes=60 << 20),
        cost_estimate=pl.CostEstimate(flops=14 * 10**9, bytes_accessed=8 * 10**6, transcendentals=0),
    )(order, owner, features, inverses, weights, residual)


def solution(mesh):
    side = {32: 4, 8: 2}[mesh.shape["rows"]]
    return jax.shard_map(
        functools.partial(body, side, mesh.shape["cls"]),
        mesh=mesh,
        in_specs=(
            P("cls", "rows", None),
            P("cls", None, None),
            P(None, "rows", "cls"),
            P("rows", "cls"),
            P(),
            P(),
        ),
        out_specs=(P(None, "rows", "cls"), P("rows", "cls")),
        check_vma=False,
    )
```
